32 devices in a mesh: dp: 8 (over y, x, core), seq: 4 (over z).
Axes of the slice: x: 2, y: 2, z: 4, core: 2. Of those that a mesh axis runs over, the one named last changes fastest.
Arguments:
- query_rows: bfloat16 [4096, 3072], P(('dp', 'seq')), parts along dimension 0, may hold values from -6 to 6
- key_rows: bfloat16 [4096, 3072], P(('dp', 'seq')), parts along dimension 0, may hold values from -6 to 6
- value_rows: bfloat16 [4096, 3072], P(('dp', 'seq')), parts along dimension 0, may hold values from -6 to 6
- query_tangent: bfloat16 [4096, 3072], P(('dp', 'seq')), parts along dimension 0, may hold values from -6 to 6
- key_tangent: bfloat16 [4096, 3072], P(('dp', 'seq')), parts along dimension 0, may hold values from -6 to 6
- value_tangent: bfloat16 [4096, 3072], P(('dp', 'seq')), parts along dimension 0, may hold values from -6 to 6
- cotangent: bfloat16 [4096, 3072], P(('dp', 'seq')), parts along dimension 0, may hold values from -6 to 6
Outputs:
- attended: bfloat16 [4096, 3072], P(('dp', 'seq')), parts along dimension 0
- attended_tangent: bfloat16 [4096, 3072], P(('dp', 'seq')), parts along dimension 0
- grad_query: bfloat16 [4096, 3072], P(('dp', 'seq')), parts along dimension 0
- grad_key: bfloat16 [4096, 3072], P(('dp', 'seq')), parts along dimension 0
- grad_value: bfloat16 [4096, 3072], P(('dp', 'seq')), parts along dimension 0
The draws below stay inside these ranges and needn't reach their ends.
There are 8 independent parts, one for each index of `dp`. The reference program is written for one: setup_inputs(seed, part) draws one part's arguments, and reference() takes and returns one part's arrays. A program takes and returns all parts, laid end to end along the dimension named above; each array names one. Nothing has to cross between parts.
All inputs are finite; a program needn't handle non-finite values.
Results may differ from the reference program's by a relative error of at most 0.0071.
Values may be sent and summed in bfloat16 or wider, within the bound.
A program may use at most 64 MiB of HBM per device.

```python
import jax
import jax.numpy as jnp
from jax import lax

HEADS = 24
HD = 128
SEQ = 512


def draw_query_rows(key, part):
    key = jax.random.fold_in(key, 11)
    base = jnp.clip(jax.random.normal(key, (SEQ, HEADS * HD), jnp.float32), -6.0, 6.0)
    return base.astype(jnp.bfloat16)


def draw_key_rows(key, part):
    key = jax.random.fold_in(key, 12)
    base = jnp.clip(jax.random.normal(key, (SEQ, HEADS * HD), jnp.float32), -6.0, 6.0)
    return base.astype(jnp.bfloat16)


def block_levels(own_key, dims, cuts, low, largest):
    level = 1.0
    for axis_at, blocks in cuts:
        draws = jax.random.uniform(jax.random.fold_in(jax.random.fold_in(own_key, 6), axis_at), (blocks,), jnp.float32, low / len(cuts), largest / len(cuts))
        level = level * jnp.repeat(jnp.exp(draws), dims[axis_at] // blocks).reshape((-1,) + (1,) * (len(dims) - 1 - axis_at))
    return level


def noise(key, shape, spread, most, shards=(), held_as=jnp.bfloat16):
    values = spread * jax.random.normal(key, shape, jnp.float32)
    if shards:
        values = values * block_levels(key, shape, shards, -0.22, 0.18)
    return jnp.clip(values, -most, most).astype(held_as)


def setup_inputs(seed: int = 0, part: int = 0) -> dict:
    seeds = jax.random.split(jax.random.key(seed), 8)
    part_keys = jax.random.split(jax.random.fold_in(seeds[7], part), 8)
    query_rows = draw_query_rows(jax.random.fold_in(jax.random.fold_in(seeds[7], part), 71), part)
    key_rows = draw_key_rows(jax.random.fold_in(jax.random.fold_in(seeds[7], part), 71), part)
    value_rows = noise(part_keys[2], (SEQ, HEADS * HD), 1.0, 6.0, ((0, 4),))
    query_tangent = noise(part_keys[3], (SEQ, HEADS * HD), 1.0, 6.0, ((0, 4),))
    key_tangent = noise(part_keys[4], (SEQ, HEADS * HD), 1.0, 6.0, ((0, 4),))
    value_tangent = noise(part_keys[5], (SEQ, HEADS * HD), 1.0, 6.0, ((0, 4),))
    cotangent = noise(part_keys[6], (SEQ, HEADS * HD), 1.0, 6.0, ((0, 4),))
    return {"query_rows": query_rows, "key_rows": key_rows, "value_rows": value_rows, "query_tangent": query_tangent, "key_tangent": key_tangent, "value_tangent": value_tangent, "cotangent": cotangent}


def probabilities(query, keys):
    scale = HD ** -0.5
    scores = jnp.dot(query, keys.T, preferred_element_type=jnp.float32) * scale
    top = jnp.max(scores, axis=-1, keepdims=True)
    expo = jnp.exp(scores - top)
    return expo / jnp.sum(expo, axis=-1, keepdims=True)


def forward_head(query, keys, values, query_tan, keys_tan, values_tan):
    scale = HD ** -0.5
    probs = probabilities(query, keys)
    probs_half = probs.astype(jnp.bfloat16)
    attended = jnp.dot(probs_half, values, preferred_element_type=jnp.float32).astype(jnp.bfloat16)
    score_tan = (jnp.dot(query_tan, keys.T, preferred_element_type=jnp.float32)
                 + jnp.dot(query, keys_tan.T, preferred_element_type=jnp.float32)) * scale
    prob_tan = probs * (score_tan - jnp.sum(probs * score_tan, axis=-1, keepdims=True))
    prob_tan = prob_tan.astype(jnp.bfloat16)
    tangent = (jnp.dot(prob_tan, values, preferred_element_type=jnp.float32)
               + jnp.dot(probs_half, values_tan, preferred_element_type=jnp.float32)).astype(jnp.bfloat16)
    return attended, tangent, probs


def backward_head(probs, query, keys, values, upstream):
    scale = HD ** -0.5
    probs_half = probs.astype(jnp.bfloat16)
    grad_values = jnp.dot(probs_half.T, upstream, preferred_element_type=jnp.float32).astype(jnp.bfloat16)
    prob_grad = jnp.dot(upstream, values.T, preferred_element_type=jnp.float32)
    score_grad = (probs * (prob_grad - jnp.sum(probs * prob_grad, axis=-1, keepdims=True)) * scale).astype(jnp.bfloat16)
    grad_q = jnp.dot(score_grad, keys, preferred_element_type=jnp.float32).astype(jnp.bfloat16)
    grad_k = jnp.dot(score_grad.T, query, preferred_element_type=jnp.float32).astype(jnp.bfloat16)
    return grad_q, grad_k, grad_values


def reference(query_rows, key_rows, value_rows, query_tangent, key_tangent, value_tangent, cotangent):
    def split(array):
        return jnp.moveaxis(array.reshape(SEQ, HEADS, HD), 1, 0)

    def per_head(items):
        query, keys, values, query_tan, keys_tan, values_tan, upstream = items
        attended, tangent, probs = forward_head(query, keys, values, query_tan, keys_tan, values_tan)
        grad_q, grad_k, grad_values = backward_head(probs, query, keys, values, upstream)
        return attended, tangent, grad_q, grad_k, grad_values

    inputs = (split(query_rows), split(key_rows), split(value_rows), split(query_tangent),
              split(key_tangent), split(value_tangent), split(cotangent))
    result = lax.map(per_head, inputs)

    def join(array):
        return jnp.moveaxis(array, 0, 1).reshape(SEQ, HEADS * HD)

    return (join(result[0]), join(result[1]), join(result[2]), join(result[3]), join(result[4]))
```

```python
import functools

import jax
import jax.numpy as jnp
from jax import lax
from jax.experimental import pallas as pl
from jax.experimental.pallas import tpu as pltpu
from jax.sharding import PartitionSpec as P

HD = 128
TILE = 256
N_IN = 7
N_OUT = 5


def dot(a, b, contract):
    return lax.dot_general(a, b, (((contract[0],), (contract[1],)), ((), ())), preferred_element_type=jnp.float32)


def attention_tile(query, query_tan, upstream, keys, values, keys_tan, values_tan):
    scale = HD ** (-0.5)
    scores = dot(query, keys, (1, 1)) * scale
    top = jnp.max(scores, axis=-1, keepdims=True)
    expo = jnp.exp(scores - top)
    probs = expo / jnp.sum(expo, axis=-1, keepdims=True)
    probs_half = probs.astype(jnp.bfloat16)
    attended = dot(probs_half, values, (1, 0))
    score_tan = (dot(query_tan, keys, (1, 1)) + dot(query, keys_tan, (1, 1))) * scale
    prob_tan = probs * (score_tan - jnp.sum(probs * score_tan, axis=-1, keepdims=True))
    prob_tan = prob_tan.astype(jnp.bfloat16)
    tangent = dot(prob_tan, values, (1, 0)) + dot(probs_half, values_tan, (1, 0))
    grad_v = dot(probs_half, upstream, (0, 0))
    prob_grad = dot(upstream, values, (1, 1))
    score_grad = probs * (prob_grad - jnp.sum(probs * prob_grad, axis=-1, keepdims=True)) * scale
    score_grad = score_grad.astype(jnp.bfloat16)
    grad_q = dot(score_grad, keys, (1, 0))
    grad_k = dot(score_grad, query, (0, 0))
    return attended, tangent, grad_q, grad_k, grad_v


def kernel(n, local, *refs):
    ins = refs[:N_IN]
    outs = refs[N_IN : N_IN + N_OUT]
    gath, made, in_send, in_recv, out_send, out_recv = refs[N_IN + N_OUT :]
    rows = ins[0].shape[0]
    total = n * rows
    tile = min(TILE, total)
    me = lax.axis_index("seq")

    barrier = pltpu.get_barrier_semaphore()
    for d in range(1, n):
        pl.semaphore_signal(
            barrier, inc=1, device_id={"seq": lax.rem(me + d, n)}, device_id_type=pl.DeviceIdType.MESH
        )
    pl.semaphore_wait(barrier, n - 1)

    mine = pl.ds(pl.multiple_of(me * rows, rows), rows)

    def columns(owner, head):
        return pl.ds(pl.multiple_of((owner * local + head) * HD, HD), HD)

    def send_inputs(head, carry):
        for d in range(1, n):
            peer = lax.rem(me + d, n)
            for a in range(N_IN):
                pltpu.make_async_remote_copy(
                    src_ref=ins[a].at[:, columns(peer, head)],
                    dst_ref=gath.at[head, a, mine, :],
                    send_sem=in_send.at[head],
                    recv_sem=in_recv.at[head],
                    device_id={"seq": peer},
                    device_id_type=pl.DeviceIdType.MESH,
                ).start()
        for a in range(N_IN):
            pltpu.make_async_copy(
                ins[a].at[:, columns(me, head)], gath.at[head, a, mine, :], in_recv.at[head]
            ).start()
        return carry

    lax.fori_loop(0, local, send_inputs, 0)

    def work(head, carry):
        pltpu.make_async_copy(gath.at[head], gath.at[head], in_recv.at[head]).wait()
        keys, values = gath[head, 1], gath[head, 2]
        keys_tan, values_tan = gath[head, 4], gath[head, 5]
        grad_k = grad_v = None
        for t in range(total // tile):
            part = pl.ds(t * tile, tile)
            attended, tangent, grad_q, more_k, more_v = attention_tile(
                gath[head, 0, part, :], gath[head, 3, part, :], gath[head, 6, part, :],
                keys, values, keys_tan, values_tan,
            )
            made[head, 0, part, :] = attended.astype(jnp.bfloat16)
            made[head, 1, part, :] = tangent.astype(jnp.bfloat16)
            made[head, 2, part, :] = grad_q.astype(jnp.bfloat16)
            grad_k = more_k if t == 0 else grad_k + more_k
            grad_v = more_v if t == 0 else grad_v + more_v
        made[head, 3] = grad_k.astype(jnp.bfloat16)
        made[head, 4] = grad_v.astype(jnp.bfloat16)
        for d in range(1, n):
            peer = lax.rem(me + d, n)
            theirs = pl.ds(pl.multiple_of(peer * rows, rows), rows)
            for o in range(N_OUT):
                pltpu.make_async_remote_copy(
                    src_ref=made.at[head, o, theirs, :],
                    dst_ref=outs[o].at[:, columns(me, head)],
                    send_sem=out_send.at[o],
                    recv_sem=out_recv.at[o],
                    device_id={"seq": peer},
                    device_id_type=pl.DeviceIdType.MESH,
                ).start()
        for o in range(N_OUT):
            pltpu.make_async_copy(
                made.at[head, o, mine, :], outs[o].at[:, columns(me, head)], out_recv.at[o]
            ).start()
        return carry

    lax.fori_loop(0, local, work, 0)

    def drain(head, carry):
        sent = gath.at[head, :, pl.ds(0, total - rows), :]
        pltpu.make_async_copy(sent, sent, in_send.at[head]).wait()
        return carry

    lax.fori_loop(0, local, drain, 0)
    for o in range(N_OUT):
        sent = outs[o].at[:, pl.ds(0, (n - 1) * local * HD)]
        pltpu.make_async_copy(sent, sent, out_send.at[o]).wait()
        pltpu.make_async_copy(outs[o], outs[o], out_recv.at[o]).wait()


def solution(mesh):
    n = mesh.shape["seq"]

    def body(*args):
        rows, width = args[0].shape
        local = width // HD // n
        return pl.pallas_call(
            functools.partial(kernel, n, local),
            out_shape=[jax.ShapeDtypeStruct((rows, width), jnp.bfloat16)] * N_OUT,
            in_specs=[pl.BlockSpec(memory_space=pl.ANY)] * N_IN,
            out_specs=[pl.BlockSpec(memory_space=pl.ANY)] * N_OUT,
            scratch_shapes=[
                pltpu.VMEM((local, N_IN, n * rows, HD), jnp.bfloat16),
                pltpu.VMEM((local, N_OUT, n * rows, HD), jnp.bfloat16),
                pltpu.SemaphoreType.DMA((local,)),
                pltpu.SemaphoreType.DMA((local,)),
                pltpu.SemaphoreType.DMA((N_OUT,)),
                pltpu.SemaphoreType.DMA((N_OUT,)),
            ],
            compiler_params=pltpu.CompilerParams(
                collective_id=0, has_side_effects=True, vmem_limit_bytes=48 * 1024 * 1024
            ),
            cost_estimate=pl.CostEstimate(
                flops=20 * local * HD * (n * rows) ** 2,
                bytes_accessed=2 * (N_IN + N_OUT) * rows * width * 2,
                transcendentals=local * (n * rows) ** 2,
            ),
        )(*args)

    spec = P(("dp", "seq"), None)
    return jax.shard_map(
        body, mesh=mesh, in_specs=(spec,) * N_IN, out_specs=(spec,) * N_OUT, check_vma=False
    )
```

```python
import functools

import jax
import jax.numpy as jnp
from jax import lax
from jax.experimental import pallas as pl
from jax.experimental.pallas import tpu as pltpu
from jax.sharding import PartitionSpec as P

HD = 128
TILE = 256
N_IN = 7
N_OUT = 5


def dot(a, b, contract):
    return lax.dot_general(a, b, (((contract[0],), (contract[1],)), ((), ())), preferred_element_type=jnp.float32)


def attention_tile(query, query_tan, upstream, keys, values, keys_tan, values_tan):
    scale = HD ** (-0.5)
    scores = dot(query, keys, (1, 1)) * scale
    top = jnp.max(scores, axis=-1, keepdims=True)
    expo = jnp.exp(scores - top)
    probs = expo / jnp.sum(expo, axis=-1, keepdims=True)
    probs_half = probs.astype(jnp.bfloat16)
    attended = dot(probs_half, values, (1, 0))
    score_tan = (dot(query_tan, keys, (1, 1)) + dot(query, keys_tan, (1, 1))) * scale
    prob_tan = probs * (score_tan - jnp.sum(probs * score_tan, axis=-1, keepdims=True))
    prob_tan = prob_tan.astype(jnp.bfloat16)
    tangent = dot(prob_tan, values, (1, 0)) + dot(probs_half, values_tan, (1, 0))
    grad_v = dot(probs_half, upstream, (0, 0))
    prob_grad = dot(upstream, values, (1, 1))
    score_grad = probs * (prob_grad - jnp.sum(probs * prob_grad, axis=-1, keepdims=True)) * scale
    score_grad = score_grad.astype(jnp.bfloat16)
    grad_q = dot(score_grad, keys, (1, 0))
    grad_k = dot(score_grad, query, (0, 0))
    return attended, tangent, grad_q, grad_k, grad_v


def partners(me, n):
    if n & (n - 1):
        return [lax.rem(me + d, n) for d in range(1, n)]
    order = []
    for d in list(range(n // 2, n)) + list(range(1, n // 2)):
        peer = me
        bit = 1
        while bit < n:
            if d & bit:
                peer = peer + bit - 2 * bit * lax.rem(lax.div(me, bit), 2)
            bit *= 2
        order.append(peer)
    return order


def place(*refs):
    done = refs[2 * N_OUT]
    copies = [pltpu.make_async_copy(refs[o], refs[N_OUT + o], done.at[o]) for o in range(N_OUT)]
    for copy in copies:
        copy.start()
    for copy in copies:
        copy.wait()


def kernel(n, local, *refs):
    ins = refs[:N_IN]
    outs = refs[N_IN : N_IN + N_OUT]
    gath, made, in_send, in_recv, out_send, out_recv = refs[N_IN + N_OUT :]
    rows = ins[0].shape[0]
    total = n * rows
    tile = min(TILE, total)
    me = lax.axis_index("seq")

    peers = partners(me, n)

    barrier = pltpu.get_barrier_semaphore()
    for peer in peers:
        pl.semaphore_signal(
            barrier, inc=1, device_id={"seq": peer}, device_id_type=pl.DeviceIdType.MESH
        )
    pl.semaphore_wait(barrier, n - 1)

    mine = pl.ds(pl.multiple_of(me * rows, rows), rows)

    def columns(owner, head):
        return pl.ds(pl.multiple_of((owner * local + head) * HD, HD), HD)

    def send_inputs(head, carry):
        for peer in peers:
            for a in range(N_IN):
                pltpu.make_async_remote_copy(
                    src_ref=ins[a].at[:, columns(peer, head)],
                    dst_ref=gath.at[head, a, mine, :],
                    send_sem=in_send.at[head],
                    recv_sem=in_recv.at[head],
                    device_id={"seq": peer},
                    device_id_type=pl.DeviceIdType.MESH,
                ).start()
        for a in range(N_IN):
            pltpu.make_async_copy(
                ins[a].at[:, columns(me, head)], gath.at[head, a, mine, :], in_recv.at[head]
            ).start()
        return carry

    lax.fori_loop(0, local, send_inputs, 0)

    def work(head, carry):
        pltpu.make_async_copy(gath.at[head], gath.at[head], in_recv.at[head]).wait()

        @pl.when(head > 0)
        def _():
            send_results(head - 1)

        keys, values = gath[head, 1], gath[head, 2]
        keys_tan, values_tan = gath[head, 4], gath[head, 5]
        grad_k = grad_v = None
        for t in range(total // tile):
            part = pl.ds(t * tile, tile)
            attended, tangent, grad_q, more_k, more_v = attention_tile(
                gath[head, 0, part, :], gath[head, 3, part, :], gath[head, 6, part, :],
                keys, values, keys_tan, values_tan,
            )
            made[head, 0, part, :] = attended.astype(jnp.bfloat16)
            made[head, 1, part, :] = tangent.astype(jnp.bfloat16)
            made[head, 2, part, :] = grad_q.astype(jnp.bfloat16)
            grad_k = more_k if t == 0 else grad_k + more_k
            grad_v = more_v if t == 0 else grad_v + more_v
        made[head, 3] = grad_k.astype(jnp.bfloat16)
        made[head, 4] = grad_v.astype(jnp.bfloat16)
        return carry

    def send_results(head):
        for peer in peers:
            theirs = pl.ds(pl.multiple_of(peer * rows, rows), rows)
            for o in range(N_OUT):
                pltpu.make_async_remote_copy(
                    src_ref=made.at[head, o, theirs, :],
                    dst_ref=outs[o].at[:, columns(me, head)],
                    send_sem=out_send.at[o],
                    recv_sem=out_recv.at[o],
                    device_id={"seq": peer},
                    device_id_type=pl.DeviceIdType.MESH,
                ).start()
        for o in range(N_OUT):
            pltpu.make_async_copy(
                made.at[head, o, mine, :], outs[o].at[:, columns(me, head)], out_recv.at[o]
            ).start()

    lax.fori_loop(0, local, work, 0)
    send_results(local - 1)

    def drain(head, carry):
        sent = gath.at[head, :, pl.ds(0, total - rows), :]
        pltpu.make_async_copy(sent, sent, in_send.at[head]).wait()
        return carry

    lax.fori_loop(0, local, drain, 0)
    for o in range(N_OUT):
        sent = outs[o].at[:, pl.ds(0, (n - 1) * local * HD)]
        pltpu.make_async_copy(sent, sent, out_send.at[o]).wait()
        pltpu.make_async_copy(outs[o], outs[o], out_recv.at[o]).wait()


def solution(mesh):
    n = mesh.shape["seq"]

    def body(*args):
        rows, width = args[0].shape
        local = width // HD // n
        results = pl.pallas_call(
            functools.partial(kernel, n, local),
            out_shape=[pltpu.VMEM((rows, width), jnp.bfloat16)] * N_OUT,
            in_specs=[pl.BlockSpec(memory_space=pl.ANY)] * N_IN,
            out_specs=[pl.BlockSpec(memory_space=pl.ANY)] * N_OUT,
            scratch_shapes=[
                pltpu.VMEM((local, N_IN, n * rows, HD), jnp.bfloat16),
                pltpu.VMEM((local, N_OUT, n * rows, HD), jnp.bfloat16),
                pltpu.SemaphoreType.DMA((local,)),
                pltpu.SemaphoreType.DMA((local,)),
                pltpu.SemaphoreType.DMA((N_OUT,)),
                pltpu.SemaphoreType.DMA((N_OUT,)),
            ],
            compiler_params=pltpu.CompilerParams(
                collective_id=0, has_side_effects=True, vmem_limit_bytes=48 * 1024 * 1024
            ),
            cost_estimate=pl.CostEstimate(
                flops=20 * local * HD * (n * rows) ** 2,
                bytes_accessed=2 * (N_IN + N_OUT) * rows * width * 2,
                transcendentals=local * (n * rows) ** 2,
            ),
        )(*[pltpu.with_memory_space_constraint(x, pltpu.HBM) for x in args])
        results = [pltpu.with_memory_space_constraint(x, pltpu.VMEM) for x in results]
        return pl.pallas_call(
            place,
            out_shape=[jax.ShapeDtypeStruct((rows, width), jnp.bfloat16)] * N_OUT,
            in_specs=[pl.BlockSpec(memory_space=pltpu.VMEM)] * N_OUT,
            out_specs=[pl.BlockSpec(memory_space=pltpu.HBM)] * N_OUT,
            scratch_shapes=[pltpu.SemaphoreType.DMA((N_OUT,))],
            compiler_params=pltpu.CompilerParams(vmem_limit_bytes=8 * 1024 * 1024),
        )(*results)

    spec = P(("dp", "seq"), None)
    return jax.shard_map(
        body, mesh=mesh, in_specs=(spec,) * N_IN, out_specs=(spec,) * N_OUT, check_vma=False
    )
```

```python
import functools

import jax
import jax.numpy as jnp
from jax import lax
from jax.experimental import pallas as pl
from jax.experimental.pallas import tpu as pltpu
from jax.sharding import PartitionSpec as P

HD = 128
TILE = 256
N_IN = 7
N_OUT = 5
GROUP = 2


def dot(a, b, contract):
    return lax.dot_general(a, b, (((contract[0],), (contract[1],)), ((), ())), preferred_element_type=jnp.float32)


def attention_tile(query, query_tan, upstream, keys, values, keys_tan, values_tan):
    scale = HD ** (-0.5)
    scores = dot(query, keys, (1, 1)) * scale
    top = jnp.max(scores, axis=-1, keepdims=True)
    expo = jnp.exp(scores - top)
    probs = expo / jnp.sum(expo, axis=-1, keepdims=True)
    probs_half = probs.astype(jnp.bfloat16)
    attended = dot(probs_half, values, (1, 0))
    score_tan = (dot(query_tan, keys, (1, 1)) + dot(query, keys_tan, (1, 1))) * scale
    prob_tan = probs * (score_tan - jnp.sum(probs * score_tan, axis=-1, keepdims=True))
    prob_tan = prob_tan.astype(jnp.bfloat16)
    tangent = dot(prob_tan, values, (1, 0)) + dot(probs_half, values_tan, (1, 0))
    grad_v = dot(probs_half, upstream, (0, 0))
    prob_grad = dot(upstream, values, (1, 1))
    score_grad = probs * (prob_grad - jnp.sum(probs * prob_grad, axis=-1, keepdims=True)) * scale
    score_grad = score_grad.astype(jnp.bfloat16)
    grad_q = dot(score_grad, keys, (1, 0))
    grad_k = dot(score_grad, query, (0, 0))
    return attended, tangent, grad_q, grad_k, grad_v


def partners(me, n):
    if n & (n - 1):
        return [lax.rem(me + d, n) for d in range(1, n)]
    order = []
    for d in list(range(n // 2, n)) + list(range(1, n // 2)):
        peer = me
        bit = 1
        while bit < n:
            if d & bit:
                peer = peer + bit - 2 * bit * lax.rem(lax.div(me, bit), 2)
            bit *= 2
        order.append(peer)
    return order


def place(*refs):
    done = refs[2 * N_OUT]
    copies = [pltpu.make_async_copy(refs[o], refs[N_OUT + o], done.at[o]) for o in range(N_OUT)]
    for copy in copies:
        copy.start()
    for copy in copies:
        copy.wait()


def kernel(n, local, group, *refs):
    ins = refs[:N_IN]
    outs = refs[N_IN : N_IN + N_OUT]
    gath, made, in_send, in_recv, out_send, out_recv = refs[N_IN + N_OUT :]
    rows = ins[0].shape[0]
    total = n * rows
    groups, wide = local // group, group * HD
    tile = min(TILE, total)
    me = lax.axis_index("seq")

    peers = partners(me, n)

    barrier = pltpu.get_barrier_semaphore()
    for peer in peers:
        pl.semaphore_signal(
            barrier, inc=1, device_id={"seq": peer}, device_id_type=pl.DeviceIdType.MESH
        )
    pl.semaphore_wait(barrier, n - 1)

    mine = pl.ds(pl.multiple_of(me * rows, rows), rows)

    def columns(owner, head):
        return pl.ds(pl.multiple_of((owner * groups + head) * wide, wide), wide)

    def send_inputs(head, carry):
        for peer in peers:
            for a in range(N_IN):
                pltpu.make_async_remote_copy(
                    src_ref=ins[a].at[:, columns(peer, head)],
                    dst_ref=gath.at[head, a, mine, :],
                    send_sem=in_send.at[head],
                    recv_sem=in_recv.at[head],
                    device_id={"seq": peer},
                    device_id_type=pl.DeviceIdType.MESH,
                ).start()
        for a in range(N_IN):
            pltpu.make_async_copy(
                ins[a].at[:, columns(me, head)], gath.at[head, a, mine, :], in_recv.at[head]
            ).start()
        return carry

    lax.fori_loop(0, groups, send_inputs, 0)

    def work(head, carry):
        pltpu.make_async_copy(gath.at[head], gath.at[head], in_recv.at[head]).wait()

        @pl.when(head > 0)
        def _():
            send_results(head - 1)

        for h in range(group):
            one = pl.ds(h * HD, HD)
            keys, values = gath[head, 1, :, one], gath[head, 2, :, one]
            keys_tan, values_tan = gath[head, 4, :, one], gath[head, 5, :, one]
            grad_k = grad_v = None
            for t in range(total // tile):
                part = pl.ds(t * tile, tile)
                attended, tangent, grad_q, more_k, more_v = attention_tile(
                    gath[head, 0, part, one], gath[head, 3, part, one], gath[head, 6, part, one],
                    keys, values, keys_tan, values_tan,
                )
                made[head, 0, part, one] = attended.astype(jnp.bfloat16)
                made[head, 1, part, one] = tangent.astype(jnp.bfloat16)
                made[head, 2, part, one] = grad_q.astype(jnp.bfloat16)
                grad_k = more_k if t == 0 else grad_k + more_k
                grad_v = more_v if t == 0 else grad_v + more_v
            made[head, 3, :, one] = grad_k.astype(jnp.bfloat16)
            made[head, 4, :, one] = grad_v.astype(jnp.bfloat16)
        return carry

    def send_results(head):
        for peer in peers:
            theirs = pl.ds(pl.multiple_of(peer * rows, rows), rows)
            for o in range(N_OUT):
                pltpu.make_async_remote_copy(
                    src_ref=made.at[head, o, theirs, :],
                    dst_ref=outs[o].at[:, columns(me, head)],
                    send_sem=out_send.at[o],
                    recv_sem=out_recv.at[o],
                    device_id={"seq": peer},
                    device_id_type=pl.DeviceIdType.MESH,
                ).start()
        for o in range(N_OUT):
            pltpu.make_async_copy(
                made.at[head, o, mine, :], outs[o].at[:, columns(me, head)], out_recv.at[o]
            ).start()

    lax.fori_loop(0, groups, work, 0)
    send_results(groups - 1)

    def drain(head, carry):
        sent = gath.at[head, :, pl.ds(0, total - rows), :]
        pltpu.make_async_copy(sent, sent, in_send.at[head]).wait()
        return carry

    lax.fori_loop(0, groups, drain, 0)
    for o in range(N_OUT):
        sent = outs[o].at[:, pl.ds(0, (n - 1) * groups * wide)]
        pltpu.make_async_copy(sent, sent, out_send.at[o]).wait()
        pltpu.make_async_copy(outs[o], outs[o], out_recv.at[o]).wait()


def solution(mesh):
    n = mesh.shape["seq"]

    def body(*args):
        rows, width = args[0].shape
        local = width // HD // n
        group = GROUP if local % GROUP == 0 else 1
        results = pl.pallas_call(
            functools.partial(kernel, n, local, group),
            out_shape=[pltpu.VMEM((rows, width), jnp.bfloat16)] * N_OUT,
            in_specs=[pl.BlockSpec(memory_space=pl.ANY)] * N_IN,
            out_specs=[pl.BlockSpec(memory_space=pl.ANY)] * N_OUT,
            scratch_shapes=[
                pltpu.VMEM((local // group, N_IN, n * rows, group * HD), jnp.bfloat16),
                pltpu.VMEM((local // group, N_OUT, n * rows, group * HD), jnp.bfloat16),
                pltpu.SemaphoreType.DMA((local // group,)),
                pltpu.SemaphoreType.DMA((local // group,)),
                pltpu.SemaphoreType.DMA((N_OUT,)),
                pltpu.SemaphoreType.DMA((N_OUT,)),
            ],
            compiler_params=pltpu.CompilerParams(
                collective_id=0, has_side_effects=True, vmem_limit_bytes=48 * 1024 * 1024
            ),
            cost_estimate=pl.CostEstimate(
                flops=20 * local * HD * (n * rows) ** 2,
                bytes_accessed=2 * (N_IN + N_OUT) * rows * width * 2,
                transcendentals=local * (n * rows) ** 2,
            ),
        )(*[pltpu.with_memory_space_constraint(x, pltpu.HBM) for x in args])
        results = [pltpu.with_memory_space_constraint(x, pltpu.VMEM) for x in results]
        return pl.pallas_call(
            place,
            out_shape=[jax.ShapeDtypeStruct((rows, width), jnp.bfloat16)] * N_OUT,
            in_specs=[pl.BlockSpec(memory_space=pltpu.VMEM)] * N_OUT,
            out_specs=[pl.BlockSpec(memory_space=pltpu.HBM)] * N_OUT,
            scratch_shapes=[pltpu.SemaphoreType.DMA((N_OUT,))],
            compiler_params=pltpu.CompilerParams(vmem_limit_bytes=8 * 1024 * 1024),
        )(*results)

    spec = P(("dp", "seq"), None)
    return jax.shard_map(
        body, mesh=mesh, in_specs=(spec,) * N_IN, out_specs=(spec,) * N_OUT, check_vma=False
    )
```
